128 devices in a mesh: subj: 4 (over y_lo, core), tile: 32 (over x, y_hi, z).
Axes of the slice: x: 4, y: 4 (y_hi: 2, y_lo: 2; y = y_hi * 2 + y_lo), z: 4, core: 2. Of those that a mesh axis runs over, the one named last changes fastest.
Arguments:
- template: float32 [8, 64, 256, 256], P(None, None, 'tile'), may hold values from -6 to 6
- images: float32 [32, 64, 256, 256], P('subj', None, 'tile'), may hold values from -6 to 6
- velocity: int32 [32, 3, 64, 256, 256], P('subj', None, None, 'tile'), may hold values from -2048 to 2047
- groups: int32 [32], P('subj'), may hold values from 0 to 7
Outputs:
- gradient: float32 [8, 64, 256, 256], P('subj', None, 'tile')
The draws below stay inside these ranges and needn't reach their ends.
All inputs are finite; a program needn't handle non-finite values.
Results may differ from the reference program's by a relative error of at most 0.00007.
Values sent between devices are 32-bit elements; how exact they have to be, the bound alone decides.
No kernel may reach another device: no remote copies, remote signals or barrier semaphores. Data moves between devices by JAX's collectives and lax.ppermute only.
A program may use at most 256 MiB of HBM per device.

```python
import jax
import jax.numpy as jnp
from jax import lax

SX = 64
NZ = 256
GROUPS = 8
SUBJECTS = 32
NY = 256


def touch_ends(array, own_key, least, top_value):
    spot = [jax.random.randint(jax.random.fold_in(own_key, axis), (), 0, length) for axis, length in enumerate(array.shape)]
    widest = array.shape.index(max(array.shape))
    next_to = spot[:widest] + [(spot[widest] + 1) % array.shape[widest]] + spot[widest + 1:]
    return array.at[tuple(spot)].set(least).at[tuple(next_to)].set(top_value)


def steps_of(rng, extent, shards, low, high):
    loudness, own = 1.0, jax.random.fold_in(rng, 6)
    for position, shards_of in shards:
        steps = jnp.exp(jax.random.uniform(jax.random.fold_in(own, position), (shards_of,), jnp.float32, low / len(shards), high / len(shards)))
        loudness = loudness * jnp.repeat(steps, extent[position] // shards_of).reshape([-1 if axis == position else 1 for axis in range(len(extent))])
    return loudness


def scatter_about(rng, shape, width, limit, pieces=(), kind=jnp.bfloat16):
    array = jax.random.normal(rng, shape, jnp.float32) * width
    if len(pieces) > 0:
        array = steps_of(rng, shape, pieces, -0.22, 0.18) * array
    return jnp.clip(array, min=-limit, max=limit).astype(kind)


def setup_inputs(seed: int = 0) -> dict:
    key_of = jax.random.split(jax.random.key(seed), 5)
    return {
        "template": scatter_about(key_of[0], (GROUPS, SX, NY, NZ), 1.0, 6.0, ((2, 32),), jnp.float32),
        "images": scatter_about(key_of[1], (SUBJECTS, SX, NY, NZ), 1.0, 6.0, ((0, 4), (2, 32)), jnp.float32),
        "velocity": touch_ends(jax.random.randint(key_of[2], (SUBJECTS, 3, SX, NY, NZ), -2048, 2048), jax.random.fold_in(key_of[2], 1), -2048, 2047).astype(jnp.int32),
        "groups": touch_ends(jax.random.randint(key_of[3], (SUBJECTS,), 0, GROUPS), jax.random.fold_in(key_of[3], 1), 0, GROUPS - 1).astype(jnp.int32),
    }


UPWIND_POS = (1.0 / 6.0, -1.0, 0.5, 1.0 / 3.0, 0.0)
UPWIND_NEG = (0.0, -1.0 / 3.0, -0.5, 1.0, -1.0 / 6.0)
VELOCITY_UNIT = 1.0 / 8192.0


def pad_along(field, along):
    widths = [(0, 0)] * field.ndim
    widths[along] = (2, 2)
    return jnp.pad(field, widths)


def stencil_valid(field, along, coeffs):
    length = field.shape[along] - 4
    result = coeffs[0] * lax.slice_in_dim(field, 0, length, axis=along)
    for shift in range(1, 5):
        result = result + coeffs[shift] * lax.slice_in_dim(field, shift, shift + length, axis=along)
    return result


def stencil_transpose(field, along, coeffs):
    length = field.shape[along] - 4
    result = coeffs[0] * lax.slice_in_dim(field, 4, 4 + length, axis=along)
    for shift in range(1, 5):
        result = result + coeffs[shift] * lax.slice_in_dim(field, 4 - shift, 4 - shift + length, axis=along)
    return result


def advance(moved_ext, speeds):
    offset = moved_ext.ndim - 3
    row_axis = offset + 1
    length = moved_ext.shape[row_axis] - 4
    middle = lax.slice_in_dim(moved_ext, 2, 2 + length, axis=row_axis)
    result = middle
    for component in range(3):
        along = offset + component
        forward_part = jnp.maximum(speeds[component], 0.0)
        backward_part = jnp.minimum(speeds[component], 0.0)
        source = moved_ext if component == 1 else pad_along(middle, along)
        result = result - forward_part * stencil_valid(source, along, UPWIND_POS)
        result = result - backward_part * stencil_valid(source, along, UPWIND_NEG)
    return result


def retreat(adjoint_mid, flux_pos, flux_neg, speeds):
    offset = adjoint_mid.ndim - 3
    result = adjoint_mid - stencil_transpose(flux_pos, offset + 1, UPWIND_POS)
    result = result - stencil_transpose(flux_neg, offset + 1, UPWIND_NEG)
    for component in (0, 2):
        along = offset + component
        forward_part = jnp.maximum(speeds[component], 0.0)
        backward_part = jnp.minimum(speeds[component], 0.0)
        result = result - stencil_transpose(pad_along(forward_part * adjoint_mid, along), along, UPWIND_POS)
        result = result - stencil_transpose(pad_along(backward_part * adjoint_mid, along), along, UPWIND_NEG)
    return result


def reference(template, images, velocity, groups):
    def one_subject(gradient, subject):
        speed_all = velocity[subject].astype(jnp.float32) * VELOCITY_UNIT
        speeds = (speed_all[0], speed_all[1], speed_all[2])
        owner = groups[subject]
        moved = template[owner]
        for substep in range(2):
            moved = advance(pad_along(moved, 1), speeds)
        adjoint = moved - images[subject]
        for substep in range(2):
            flux_pos = pad_along(jnp.maximum(speeds[1], 0.0) * adjoint, 1)
            flux_neg = pad_along(jnp.minimum(speeds[1], 0.0) * adjoint, 1)
            adjoint = retreat(adjoint, flux_pos, flux_neg, speeds)
        return gradient.at[owner].add(adjoint), None

    initial = jnp.zeros(template.shape, jnp.float32)
    gradient, unused = lax.scan(one_subject, initial, jnp.arange(SUBJECTS, dtype=jnp.int32))
    return gradient
```

```python
import functools

import jax
import jax.numpy as jnp
from jax import lax
from jax.experimental import pallas as pl
from jax.experimental.pallas import tpu as pltpu
from jax.sharding import PartitionSpec as P

SCALE = 1.0 / (6.0 * 8192.0)
SX = 64
ROWS = 8
NZ = 256
HALF = 128
SUBS = 8
GROUPS = 8
CUTS = (36,)
VMEM = 48 * 1024 * 1024
UNROLL = 4


def bounds(shift):
    return [0] + [cut - shift for cut in CUTS] + [SX]


def spec(shape, index):
    return pl.BlockSpec(tuple(pl.Element(size) for size in shape), index)


def lanes(value, shift, lane):
    low, high = value[:, :HALF], value[:, HALF:]
    roll_low, roll_high = pltpu.roll(low, shift % HALF, 1), pltpu.roll(high, shift % HALF, 1)
    if shift > 0:
        mask = lane < shift
        first = jnp.where(mask, 0.0, roll_low)
        second = jnp.where(mask, roll_low, roll_high)
    else:
        mask = lane >= HALF + shift
        first = jnp.where(mask, roll_high, roll_low)
        second = jnp.where(mask, 0.0, roll_high)
    return jnp.concatenate([first, second], axis=1)


def rows(value, shift):
    return pltpu.roll(value, shift % ROWS, 0)


def iotas():
    row = lax.broadcasted_iota(jnp.int32, (ROWS, NZ), 0)
    lane = lax.broadcasted_iota(jnp.int32, (ROWS, HALF), 1)
    return row, lane


def frame(upper, lower):
    return jnp.concatenate([upper, jnp.zeros((ROWS - 4, NZ), jnp.float32), lower], axis=0)


def upwind(speed, back2, back1, mid3, fore1, fore2):
    speed = speed.astype(jnp.float32)
    forward = speed > 0.0
    near = jnp.where(forward, back1, fore1)
    far = jnp.where(forward, back2, fore2)
    ahead = jnp.where(forward, fore1, back1)
    return jnp.abs(speed) * (far - 6.0 * near + mid3 + (ahead + ahead))


def advance_slice(get, x, halo, speed, masks):
    row, lane = masks
    zero = jnp.zeros((ROWS, NZ), jnp.float32)

    def at(position):
        value = get(position)
        return zero if value is None else value

    mid = get(x)
    mid3 = 3.0 * mid
    change = upwind(speed[0], at(x - 2), at(x - 1), mid3, at(x + 1), at(x + 2))
    back1 = rows(jnp.where(row == 7, halo, mid), 1)
    back2 = rows(jnp.where(row >= 6, halo, mid), 2)
    fore1 = rows(jnp.where(row == 0, halo, mid), -1)
    fore2 = rows(jnp.where(row <= 1, halo, mid), -2)
    change = change + upwind(speed[1], back2, back1, mid3, fore1, fore2)
    back1, back2 = lanes(mid, 1, lane), lanes(mid, 2, lane)
    fore1, fore2 = lanes(mid, -1, lane), lanes(mid, -2, lane)
    change = change + upwind(speed[2], back2, back1, mid3, fore1, fore2)
    return mid - SCALE * change


def parts(speed, twice):
    speed = speed.astype(jnp.float32)
    pos = jnp.maximum(speed, 0.0) * twice
    neg = jnp.minimum(speed, 0.0) * twice
    pos3, neg3 = 3.0 * pos, 3.0 * neg
    return 0.5 * pos, -(pos3 + neg), pos - neg, pos + neg3, -0.5 * neg


def scatter_rows(speed, twice, row):
    plus2, plus1, middle, minus1, minus2 = parts(speed, twice)
    step = rows(plus2, -1)
    out_far = step[7:8]
    step = rows(plus1 + jnp.where(row < 7, step, 0.0), -1)
    out_near = step[7:8]
    change = jnp.where(row < 7, step, 0.0)
    step = rows(minus2, 1)
    in_far = step[0:1]
    step = rows(minus1 + jnp.where(row > 0, step, 0.0), 1)
    in_near = step[0:1]
    change = change + jnp.where(row > 0, step, 0.0)
    return change, middle, (out_far, out_near), (in_near, in_far)


def scatter_lanes(speed, twice, lane):
    plus2, plus1, middle, minus1, minus2 = parts(speed, twice)
    change = lanes(plus1 + lanes(plus2, -1, lane), -1, lane)
    change = change + lanes(minus1 + lanes(minus2, 1, lane), 1, lane)
    return change, middle


def loop(start, stop, body, carry):
    whole = (stop - start) // UNROLL

    def several(step, carry):
        for k in range(UNROLL):
            carry = body(start + step * UNROLL + k, carry)
        return carry

    if whole > 0:
        carry = lax.fori_loop(0, whole, several, carry)
    for x in range(start + whole * UNROLL, stop):
        carry = body(x, carry)
    return carry


def getter(main, main_low, main_high, tail=None, tail_low=0):
    def get(x):
        if isinstance(x, int):
            if x < 0 or x >= SX:
                return None
            if x < main_low:
                return tail[0, x - tail_low]
        return main[0, x - main_low]

    return get


def walk(low, high, main_low, main_high, body):
    first = min(max(low, main_low + 2), high)
    last = max(min(high, main_high - 2), first)
    for x in range(low, first):
        body(x, 0)
    loop(first, last, lambda x, carry: (body(x, carry), carry)[1], 0)
    for x in range(last, high):
        body(x, 0)


def first_kernel(low, high, in_low, in_high, groups, side, template, prev_own, prev_other, next_own, next_other,
                 velocity, moved, up, down):
    masks = iotas()
    own = (groups[pl.program_id(0)] // (GROUPS // 2)) == side[0]
    get = getter(template, in_low, in_high)

    def body(x, carry):
        k = x - low
        upper = jnp.where(own, next_own[0, k], next_other[0, k])
        lower = jnp.where(own, prev_own[0, k], prev_other[0, k])
        speed = [velocity[0, d, k] for d in range(3)]
        value = advance_slice(get, x, frame(upper, lower), speed, masks)
        moved[0, k] = value
        up[0, k] = value[0:2]
        down[0, k] = value[6:8]

    walk(low, high, in_low, in_high, body)


def second_kernel(low, high, in_low, in_high, tail_low, *refs):
    if tail_low is None:
        moved, prev, next_, velocity, images, residual, up, down = refs
        tail = None
    else:
        tail, moved, prev, next_, velocity, images, residual, up, down = refs
    masks = iotas()
    get = getter(moved, in_low, in_high, tail, tail_low)

    def body(x, carry):
        k = x - low
        speed = [velocity[0, d, k] for d in range(3)]
        value = advance_slice(get, x, frame(next_[0, k], prev[0, k]), speed, masks)
        value = value - images[0, k]
        residual[0, k] = value
        _, _, out, into = scatter_rows(speed[1], value + value, masks[0])
        up[0, k, 0:1] = out[0]
        up[0, k, 1:2] = out[1]
        down[0, k, 0:1] = into[0]
        down[0, k, 1:2] = into[1]

    walk(low, high, in_low, in_high, body)


def scatter_walk(low, high, get, speed_of, extra, emit, edges, masks, loop_low):
    zero = jnp.zeros((ROWS, NZ), jnp.float32)
    row, lane = masks

    def body(x, carry, inside=True, last=True):
        now0, now1, now2, now3 = carry
        value = get(x)
        twice = value + value
        speed = speed_of(x)
        plus2, plus1, middle, minus1, minus2 = parts(speed[0], twice)
        if not isinstance(x, int) or x >= low + 2:
            done = get(x - 2) - SCALE * (now0 + plus2)
            emit(x - 2, done)
        if inside:
            ychange, ymiddle, out, into = scatter_rows(speed[1], twice, row)
            zchange, zmiddle = scatter_lanes(speed[2], twice, lane)
            own = (ychange + zchange) + 1.5 * (middle + ymiddle + zmiddle)
            if extra is not None:
                own = own + extra(x)
            if edges is not None:
                edges(x, out, into)
            now2 = now2 + own
        return now1 + plus1, now2, now3 + minus1, minus2

    carry = (zero,) * 4
    start = max(low - 2, 0)
    stop = min(high + 2, SX)
    first = min(max(loop_low, low + 2), high)
    for x in range(start, first):
        carry = body(x, carry, inside=low <= x < high)
    carry = loop(first, high, body, carry)
    for x in range(high, stop):
        carry = body(x, carry, inside=False)
    if high == SX:
        for x, change in ((SX - 2, carry[0]), (SX - 1, carry[1])):
            emit(x, get(x) - SCALE * change)


def third_kernel(low3, high3, low4, high4, in_low, vel_low, tail_low, keep_low, groups, side, *refs):
    refs = list(refs)
    tail = before = None
    if tail_low is not None:
        tail, before = refs[:2]
        refs = refs[2:]
    main, prev, next_, velocity, sums, edges = refs[:6]
    refs = refs[6:]
    keep = refs.pop(0) if keep_low is not None else None
    (adjoint,) = refs
    masks = iotas()
    s = pl.program_id(0)
    group = groups[s]
    owner = group // 2
    core = (owner % 2 == side[0]).astype(jnp.int32)
    slot = core * 4 + (owner // 2 == side[1]).astype(jnp.int32) * 2 + group % 2

    @pl.when(s == 0)
    def clear():
        sums[...] = jnp.zeros_like(sums)
        edges[...] = jnp.zeros_like(edges)

    get = getter(main, in_low, SX, tail, tail_low)
    base = low4 - 2 if low4 > 0 else 0
    if before is not None:
        for x in range(base, low3):
            adjoint[0, x - base] = before[0, x - base]

    def speed_of(x):
        return [velocity[0, d, x - vel_low] for d in range(3)]

    def extra(x):
        k = x - low3
        upper = prev[0, k]
        lower = next_[0, k]
        return frame(upper, lower)

    def emit(x, value):
        adjoint[0, x - base] = value

    scatter_walk(low3, high3, get, speed_of, extra, emit, None, masks, in_low + 2)
    if keep is not None:
        for x in range(keep_low, high3):
            keep[0, x - keep_low] = adjoint[0, x - base]

    def emit_sum(x, value):
        k = x - low4
        sums[slot, k] = sums[slot, k] + value

    def emit_edges(x, out, into):
        k = x - low4
        block = jnp.concatenate([out[0], out[1], into[0], into[1]], axis=0)
        edges[slot, k] = edges[slot, k] - SCALE * block

    get4 = getter(adjoint, base, SX)
    scatter_walk(low4, high4, get4, speed_of, None, emit_sum, emit_edges, masks, low4 + 2)


def call(body, grid, scalars, ins, outs, arrays, scratch=(), flops=0):
    nbytes = sum(a.size * 4 for a in arrays)
    return pl.pallas_call(
        body,
        grid_spec=pltpu.PrefetchScalarGridSpec(
            num_scalar_prefetch=len(scalars),
            grid=grid,
            in_specs=ins,
            out_specs=[o[1] for o in outs],
            scratch_shapes=list(scratch),
        ),
        out_shape=[jax.ShapeDtypeStruct(o[0], jnp.float32) for o in outs],
        compiler_params=pltpu.CompilerParams(vmem_limit_bytes=VMEM, dimension_semantics=("arbitrary",)),
        cost_estimate=pl.CostEstimate(flops=flops, bytes_accessed=nbytes, transcendentals=0),
    )(*scalars, *arrays)


def subject(*tail):
    return lambda s, *scalars: (s,) + tail


def neighbours(up, down, count):
    from_next = lax.ppermute(up, "tile", [(i + 1, i) for i in range(count - 1)])
    from_prev = lax.ppermute(down, "tile", [(i, i + 1) for i in range(count - 1)])
    return from_prev, from_next


def shards(template, images, velocity, groups):
    count = lax.axis_size("tile")
    place = lax.axis_index("subj")
    core, high_y = place % 2, place // 2
    half = GROUPS // 2
    core_pairs = [(0, 1), (1, 0), (2, 3), (3, 2)]
    y_pairs = [(0, 2), (2, 0), (1, 3), (3, 1)]
    side = jnp.stack([core, high_y]).astype(jnp.int32)
    chunks = len(CUTS) + 1

    mine = lax.dynamic_slice_in_dim(template, core * half, half, axis=0)
    prev_own, next_own = neighbours(mine[:, :, 0:2], mine[:, :, 6:8], count)
    both = lax.ppermute(jnp.stack([prev_own, next_own]), "subj", core_pairs)
    prev_other, next_other = both[0], both[1]

    field = lambda n: (SUBS, n, ROWS, NZ)
    edge = lambda n: (SUBS, n, 2, NZ)

    b1, b2, b3, b4 = (bounds(2 * k) for k in range(4))
    moved, moved_edges = [], []
    for c in range(chunks):
        low, high = b1[c], b1[c + 1]
        n = high - low
        in_low, in_high = max(low - 2, 0), min(high + 2, SX)
        halo_spec = spec((1, n, 2, NZ), lambda s, g, d, low=low: (g[s] % half, low, 0, 0))
        out = call(
            functools.partial(first_kernel, low, high, in_low, in_high),
            (SUBS,),
            (groups, side),
            [spec((1, in_high - in_low, ROWS, NZ), lambda s, g, d, in_low=in_low: (g[s], in_low, 0, 0))]
            + [halo_spec] * 4
            + [spec((1, 3, n, ROWS, NZ), subject(0, low, 0, 0))],
            [(field(n), spec((1, n, ROWS, NZ), subject(0, 0, 0)))]
            + [(edge(n), spec((1, n, 2, NZ), subject(0, 0, 0)))] * 2,
            (template, prev_own, prev_other, next_own, next_other, velocity),
            flops=50 * SUBS * n * ROWS * NZ,
        )
        moved.append(out[0])
        moved_edges.append(neighbours(out[1], out[2], count))

    residual, residual_edges = [], []
    for c in range(chunks):
        low, high = b2[c], b2[c + 1]
        n = high - low
        main_low, main_high = b1[c], b1[c + 1]
        m = main_high - main_low
        ins, arrays, tail_low = [], (), None
        if c > 0:
            tail_low = main_low - 4
            before_low = b1[c - 1]
            ins.append(spec((1, 4, ROWS, NZ), subject(tail_low - before_low, 0, 0)))
            arrays += (moved[c - 1],)
        prev, next_ = moved_edges[c]
        if c > 0:
            back = main_low - low
            prev = jnp.concatenate([moved_edges[c - 1][0][:, -back:], prev], axis=1)
            next_ = jnp.concatenate([moved_edges[c - 1][1][:, -back:], next_], axis=1)
        ins += [
            spec((1, m, ROWS, NZ), subject(0, 0, 0)),
            spec((1, n, 2, NZ), subject(0, 0, 0)),
            spec((1, n, 2, NZ), subject(0, 0, 0)),
            spec((1, 3, n, ROWS, NZ), subject(0, low, 0, 0)),
            spec((1, n, ROWS, NZ), subject(low, 0, 0)),
        ]
        arrays += (moved[c], prev, next_, velocity, images)
        out = call(
            functools.partial(second_kernel, low, high, main_low, main_high, tail_low),
            (SUBS,),
            (),
            ins,
            [(field(n), spec((1, n, ROWS, NZ), subject(0, 0, 0)))]
            + [(edge(n), spec((1, n, 2, NZ), subject(0, 0, 0)))] * 2,
            arrays,
            flops=60 * SUBS * n * ROWS * NZ,
        )
        residual.append(out[0])
        residual_edges.append(neighbours(out[1], out[2], count))

    results, kept = [], None
    for c in range(chunks):
        low3, high3, low4, high4 = b3[c], b3[c + 1], b4[c], b4[c + 1]
        n3, n4 = high3 - low3, high4 - low4
        main_low, main_high = b2[c], b2[c + 1]
        m = main_high - main_low
        ins, arrays, tail_low = [], (), None
        prev, next_ = residual_edges[c]
        if c > 0:
            tail_low = main_low - 4
            ins.append(spec((1, 4, ROWS, NZ), subject(tail_low - b2[c - 1], 0, 0)))
            ins.append(spec((1, 4, ROWS, NZ), subject(0, 0, 0)))
            arrays += (residual[c - 1], kept)
            back = main_low - low3
            prev = jnp.concatenate([residual_edges[c - 1][0][:, -back:], prev], axis=1)
            next_ = jnp.concatenate([residual_edges[c - 1][1][:, -back:], next_], axis=1)
        base = max(low4 - 2, 0)
        vel_low, vel_high = base, min(high3 + 2, SX)
        vn = vel_high - vel_low
        ins += [
            spec((1, m, ROWS, NZ), subject(0, 0, 0)),
            spec((1, n3, 2, NZ), subject(0, 0, 0)),
            spec((1, n3, 2, NZ), subject(0, 0, 0)),
            spec((1, 3, vn, ROWS, NZ), subject(0, vel_low, 0, 0)),
        ]
        arrays += (residual[c], prev, next_, velocity)
        outs = [
            ((GROUPS, n4, ROWS, NZ), spec((GROUPS, n4, ROWS, NZ), lambda s, *r: (0, 0, 0, 0))),
            ((GROUPS, n4, 4, NZ), spec((GROUPS, n4, 4, NZ), lambda s, *r: (0, 0, 0, 0))),
        ]
        keep_low = None
        if c + 1 < chunks:
            keep_low = high4 - 2
            outs.append(((SUBS, 4, ROWS, NZ), spec((1, 4, ROWS, NZ), subject(0, 0, 0))))
        out = call(
            functools.partial(third_kernel, low3, high3, low4, high4, main_low, vel_low, tail_low, keep_low),
            (SUBS,),
            (groups, side),
            ins,
            outs,
            arrays,
            scratch=[pltpu.VMEM((1, high3 - base, ROWS, NZ), jnp.float32)],
            flops=130 * SUBS * n4 * ROWS * NZ,
        )
        if keep_low is not None:
            kept = out[2]
        sums, edges = out[0], out[1]
        sums4 = sums[half:] + lax.ppermute(sums[:half], "subj", core_pairs)
        edges4 = edges[half:] + lax.ppermute(edges[:half], "subj", core_pairs)
        sums2 = sums4[2:] + lax.ppermute(sums4[:2], "subj", y_pairs)
        edges2 = edges4[2:] + lax.ppermute(edges4[:2], "subj", y_pairs)
        from_prev, from_next = neighbours(edges2[:, :, 0:2], edges2[:, :, 2:4], count)
        middle = jnp.zeros((2, n4, ROWS - 4, NZ), jnp.float32)
        results.append(sums2 + jnp.concatenate([from_prev, middle, from_next], axis=2))
    return jnp.concatenate(results, axis=1)


def solution(mesh):
    in_specs = (
        P(None, None, "tile", None),
        P("subj", None, "tile", None),
        P("subj", None, None, "tile", None),
        P("subj"),
    )
    out_specs = P("subj", None, "tile", None)
    return jax.shard_map(shards, mesh=mesh, in_specs=in_specs, out_specs=out_specs, check_vma=False)
```

```python
import functools

import jax
import jax.numpy as jnp
import numpy as np
from jax import lax
from jax.experimental import pallas as pl
from jax.experimental.pallas import tpu as pltpu
from jax.sharding import PartitionSpec as P

SCALE = 1.0 / (6.0 * 8192.0)
SX = 64
ROWS = 8
NZ = 256
HALF = 128
SUBS = 8
GROUPS = 8
CUTS = (24, 48)
VMEM = 12 * 1024 * 1024
STREAMING = 40 * 1024 * 1024
UNROLL = 4
STRIDE = 16
PLUS = {-2: 1.0, -1: -6.0, 0: 3.0, 1: 2.0}
MINUS = {-1: -2.0, 0: -3.0, 1: 6.0, 2: -1.0}


def padded(n):
    return (n + 7) // 8 * 8


def stencil(taps):
    matrix = np.zeros((NZ, NZ), np.float32)
    for shift, weight in taps.items():
        matrix += weight * np.eye(NZ, k=shift, dtype=np.float32)
    return matrix


def half(h):
    return slice(h * HALF, (h + 1) * HALF)


def eights(start):
    return pl.ds(start if isinstance(start, int) else pl.multiple_of(start, ROWS), ROWS)


def loop(count, body, step=UNROLL, first=0):
    for k in range(first):
        body(k)
    whole = (count - first) // step

    def several(block, carry):
        for k in range(step):
            body(first + block * step + k)
        return carry

    if whole > 0:
        lax.fori_loop(0, whole, several, 0)
    for k in range(first + whole * step, count):
        body(k)


class Padded:
    def __init__(self, ref, low):
        self.ref, self.low = ref, low

    def start(self, x):
        return (x - self.low) * STRIDE + ROWS

    def read(self, h, x, shift=0):
        start = self.start(x)
        return self.ref[h, eights(start) if shift == 0 else pl.ds(start + shift, ROWS), :]

    def write(self, h, x, value):
        self.ref[h, eights(self.start(x)), :] = value

    def every(self, x, row):
        return pl.ds(self.start(x) + row, ROWS, stride=STRIDE)


def pad_rows(slices):
    return (2, slices * STRIDE + 2 * ROWS, HALF)


def upwind(speed, back2, back1, mid3, fore1, fore2):
    speed = speed.astype(jnp.float32)
    forward = speed > 0.0
    near = jnp.where(forward, back1, fore1)
    far = jnp.where(forward, back2, fore2)
    ahead = jnp.where(forward, fore1, back1)
    return jnp.abs(speed) * (far - 6.0 * near + mid3 + (ahead + ahead))


def split(value):
    high = value.astype(jnp.bfloat16)
    return high, (value - high.astype(jnp.float32)).astype(jnp.bfloat16)


def fill(field, ref):
    def body(x):
        for h in range(2):
            field.write(h, x, ref[0, x, :, half(h)])

    loop(SX, body)


def clear(ref):
    ref[...] = jnp.zeros_like(ref)


def every(x, row):
    return pl.ds(x * ROWS + row, ROWS, stride=ROWS)


def of(x):
    return eights(x * ROWS)


def put_rows(dst, top, bottom, low, high, base):
    for x in range(low, high, ROWS):
        for h in range(2):
            for r in range(2):
                dst[h, every(x - base, r), :] = top[0, r, x:x + ROWS, half(h)]
                dst[h, every(x - base, 6 + r), :] = bottom[0, r, x:x + ROWS, half(h)]


def advance(field, velocity, weights, lhs, along, emit):
    def halves(k):
        x = k * 2
        for h in range(2):
            pair = jnp.concatenate([field.read(h, x), field.read(h, x + 1)], axis=0)
            high, rest = split(pair)
            rows = pl.ds(k * 16 if isinstance(k, int) else pl.multiple_of(k * 16, 16), 16)
            lhs[rows, half(h)] = high
            lhs[rows, half(2 + h)] = rest

    loop(SX // 2, halves, UNROLL // 2)
    along[...] = jnp.dot(lhs[...], weights[...], preferred_element_type=jnp.float32)

    def body(x):
        for h in range(2):
            mid = field.read(h, x)
            mid3 = 3.0 * mid
            speed = [velocity[0, d, x, :, half(h)] for d in range(3)]
            change = upwind(speed[0], *(field.read(h, x + s) if s else mid3 for s in (-2, -1, 0, 1, 2)))
            change += upwind(speed[1], *(field.read(h, x, s) if s else mid3 for s in (-2, -1, 0, 1, 2)))
            ahead = speed[2].astype(jnp.float32)
            plus, minus = along[of(x), half(h)], along[of(x), half(2 + h)]
            change += ahead * jnp.where(ahead > 0.0, plus, minus)
            emit(h, x, mid - SCALE * change, speed)

    loop(SX, body)


def first_kernel(s, groups, template, weights, moved, sides, pad, speeds, lhs, along, velocity):
    @pl.when(s == 0)
    def start():
        clear(pad)

    field = Padded(pad, -2)
    fill(field, template)

    def emit(h, x, value, speed):
        moved[0, h, of(x), :] = value
        speeds[h, of(x), :] = speed[1].astype(jnp.float32)

    advance(field, velocity, weights, lhs, along, emit)
    for x in range(0, SX, ROWS):
        for h in range(2):
            for i, r in enumerate((0, 1, 6, 7)):
                sides[0, i, x:x + ROWS, half(h)] = speeds[h, every(x, r), :]


def entering(value, speed, prev, next_, k, h):
    group = slice(k, k + ROWS)
    back2, back1 = prev[0, 0, group, half(h)], prev[0, 1, group, half(h)]
    fore1, fore2 = next_[0, 0, group, half(h)], next_[0, 1, group, half(h)]
    v0, v1, v6, v7 = (speed[0, i, group, half(h)] for i in range(4))
    change = (
        jnp.abs(v0) * jnp.where(v0 > 0.0, back2 - 6.0 * back1, 2.0 * back1),
        jnp.maximum(v1, 0.0) * back1,
        jnp.maximum(-v6, 0.0) * fore1,
        jnp.abs(v7) * jnp.where(v7 > 0.0, 2.0 * fore1, fore2 - 6.0 * fore1),
    )
    return [value[0, h, every(k, r), :] - SCALE * c for r, c in zip((0, 1, 6, 7), change)]


class Picked:
    def __init__(self, yes, first, second):
        self.yes, self.first, self.second = yes, first, second

    def __getitem__(self, index):
        return jnp.where(self.yes, self.first[index], self.second[index])


def arrivals(side, even, odd):
    yes = side[2] == 1
    return Picked(yes, even, odd), Picked(yes, odd, even)


def departures(side, both):
    return both.at[1 - side[2]], both.at[side[2]]


def first_border(s, groups, side, moved, even_own, even_other, odd_own, odd_other, sides, both):
    own = (groups[s] // (GROUPS // 2)) == side[0]
    up, down = departures(side, both)

    def finish(even, odd):
        prev, next_ = arrivals(side, even, odd)
        for k in range(0, SX, ROWS):
            for h in range(2):
                rows = entering(moved, sides, prev, next_, k, h)
                for r in range(2):
                    up[0, r, k:k + ROWS, half(h)] = rows[r]
                    down[0, r, k:k + ROWS, half(h)] = rows[2 + r]

    @pl.when(own)
    def from_own():
        finish(even_own, odd_own)

    @pl.when(jnp.logical_not(own))
    def from_other():
        finish(even_other, odd_other)


def second_kernel(s, groups, side, moved, both, images, weights, residual, pad, lhs, along, velocity):
    @pl.when(s == 0)
    def start():
        clear(pad)

    field = Padded(pad, -2)
    up, down = departures(side, both)

    def copy(x):
        for h in range(2):
            field.write(h, x, moved[0, h, of(x), :])

    loop(SX, copy)
    for x in range(0, SX, ROWS):
        for h in range(2):
            for r in range(2):
                pad[h, field.every(x, r), :] = up[0, r, x:x + ROWS, half(h)]
                pad[h, field.every(x, 6 + r), :] = down[0, r, x:x + ROWS, half(h)]

    def emit(h, x, value, speed):
        residual[0, h, of(x), :] = value - images[0, x, :, half(h)]

    advance(field, velocity, weights, lhs, along, emit)


def second_border(s, groups, side, residual, even, odd, sides, top, bottom, both):
    prev, next_ = arrivals(side, even, odd)
    up, down = departures(side, both)
    for k in range(0, SX, ROWS):
        group = slice(k, k + ROWS)
        for h in range(2):
            rows = dict(zip((0, 1, 6, 7), entering(residual, sides, prev, next_, k, h)))
            speed = dict(zip((0, 1, 6, 7), (sides[0, i, group, half(h)] for i in range(4))))
            for r in range(2):
                top[0, r, group, half(h)] = rows[r]
                bottom[0, r, group, half(h)] = rows[6 + r]
            pos = {r: jnp.maximum(speed[r], 0.0) * rows[r] for r in (0, 1, 7)}
            neg = {r: jnp.minimum(speed[r], 0.0) * rows[r] for r in (0, 6, 7)}
            for ref, r, change in outgoing(pos, neg):
                (up, down)[ref][0, r, group, half(h)] = change


def outgoing(pos, neg):
    return (
        (0, 0, -SCALE * pos[0]),
        (0, 1, -SCALE * (pos[1] - 6.0 * pos[0] - 2.0 * neg[0])),
        (1, 0, -SCALE * (2.0 * pos[7] + 6.0 * neg[7] - neg[6])),
        (1, 1, SCALE * neg[7]),
    )


def retreat(low, high, value, base, near, velocity, emit, weights, pos_pad, neg_pad, lhs, along):
    def get(h, x):
        return value[h, of(x - base), :]

    def speed_of(d, h, x):
        return velocity[0, d, x - near, :, half(h)]

    n = high - low
    pos_field, neg_field = Padded(pos_pad, low), Padded(neg_pad, low)

    def before(k):
        x = low + k * 2
        rows = pl.ds(k * 16 if isinstance(k, int) else pl.multiple_of(k * 16, 16), 16)
        for h in range(2):
            pairs = []
            for i in range(2):
                here = get(h, x + i)
                speed = speed_of(1, h, x + i).astype(jnp.float32)
                pos_field.write(h, x + i, jnp.maximum(speed, 0.0) * here)
                neg_field.write(h, x + i, jnp.minimum(speed, 0.0) * here)
                speed = speed_of(2, h, x + i).astype(jnp.float32)
                pairs.append((jnp.maximum(speed, 0.0) * here, jnp.minimum(speed, 0.0) * here))
            for j in range(2):
                top, rest = split(jnp.concatenate([pairs[0][j], pairs[1][j]], axis=0))
                lhs[rows, half(4 * j + h)] = top
                lhs[rows, half(4 * j + 2 + h)] = rest

    loop(n // 2, before, UNROLL // 2)
    along[...] = jnp.dot(lhs[...], weights[...], preferred_element_type=jnp.float32)

    def one(h, x, carry, inside):
        now0, now1, now2, now3 = carry
        here = get(h, x)
        twice = here + here
        speed = speed_of(0, h, x).astype(jnp.float32)
        pos, neg = jnp.maximum(speed, 0.0) * twice, jnp.minimum(speed, 0.0) * twice
        if not isinstance(x, int) or x >= low + 2:
            emit(h, x - 2, get(h, x - 2) - SCALE * (now0 + 0.5 * pos))
        if inside:
            ypos, yneg = pos_field.read(h, x), neg_field.read(h, x)
            own = pos_field.read(h, x, 2) - neg_field.read(h, x, -2)
            own += 2.0 * (pos_field.read(h, x, -1) - neg_field.read(h, x, 1))
            own -= 6.0 * (pos_field.read(h, x, 1) - neg_field.read(h, x, -1))
            own += 3.0 * (ypos - yneg) + 1.5 * (pos - neg)
            own += along[eights((x - low) * ROWS), half(h)]
            now2 = now2 + own
        return now1 - (3.0 * pos + neg), now2, now3 + (pos + 3.0 * neg), -0.5 * neg

    def body(x, carry, inside=True):
        return tuple(one(h, x, carry[h], inside) for h in range(2))

    zero = jnp.zeros((ROWS, HALF), jnp.float32)
    carry = ((zero,) * 4,) * 2
    first, last = low + 2, high
    for x in range(max(low - 2, 0), first):
        carry = body(x, carry, low <= x)
    whole = (last - first) // UNROLL

    def several(block, carry):
        for k in range(UNROLL):
            carry = body(first + block * UNROLL + k, carry)
        return carry

    carry = lax.fori_loop(0, whole, several, carry)
    for x in range(first + whole * UNROLL, last):
        carry = body(x, carry)
    for x in range(last, min(high + 2, SX)):
        carry = body(x, carry, False)
    if high == SX:
        for h in range(2):
            emit(h, SX - 2, get(h, SX - 2) - SCALE * carry[h][0])
            emit(h, SX - 1, get(h, SX - 1) - SCALE * carry[h][1])


def third_kernel(s, groups, residual, top, bottom, weights, adjoint, value, pos_pad, neg_pad, lhs, along, velocity):
    @pl.when(s == 0)
    def start():
        clear(pos_pad)
        clear(neg_pad)

    def copy(x):
        for h in range(2):
            value[h, of(x), :] = residual[0, h, of(x), :]

    loop(SX, copy)
    put_rows(value, top, bottom, 0, SX, 0)

    def emit(h, x, result):
        adjoint[0, h, of(x), :] = result

    retreat(0, SX, value, 0, 0, velocity, emit, weights, pos_pad, neg_pad, lhs, along)


def slot_of(group, side):
    owner = group // 2
    core = (owner % 2 == side[0]).astype(jnp.int32)
    return core * 4 + (owner // 2 == side[1]).astype(jnp.int32) * 2 + group % 2


def third_border(s, groups, side, adjoint, even, odd, sides, edges):
    prev, next_ = arrivals(side, even, odd)
    slot = slot_of(groups[s], side)

    @pl.when(s == 0)
    def start():
        clear(edges)

    for k in range(0, SX, ROWS):
        group = slice(k, k + ROWS)
        for h in range(2):
            value = {r: adjoint[0, h, every(k, r), :] + prev[0, r, group, half(h)] for r in (0, 1)}
            value.update({6 + r: adjoint[0, h, every(k, 6 + r), :] + next_[0, r, group, half(h)] for r in (0, 1)})
            speed = dict(zip((0, 1, 6, 7), (sides[0, i, group, half(h)] for i in range(4))))
            pos = {r: jnp.maximum(speed[r], 0.0) * value[r] for r in (0, 1, 7)}
            neg = {r: jnp.minimum(speed[r], 0.0) * value[r] for r in (0, 6, 7)}
            for ref, r, change in outgoing(pos, neg):
                at = (2 * ref + r) * SX + k
                edges[slot, at:at + ROWS, half(h)] += change


def fourth_kernel(low, high, near, s, groups, side, adjoint, even, odd, weights, sums,
                  value, pos_pad, neg_pad, lhs, along, velocity):
    prev, next_ = arrivals(side, even, odd)
    slot = slot_of(groups[s], side)

    @pl.when(s == 0)
    def start():
        for ref in (sums, pos_pad, neg_pad):
            clear(ref)

    base, stop = max(low - 8, 0), min(high + 8, SX)

    def copy(k):
        for h in range(2):
            value[h, of(k), :] = adjoint[0, h, of(base + k), :]

    loop(stop - base, copy)
    for x in range(base, stop, ROWS):
        for h in range(2):
            for r in range(2):
                value[h, every(x - base, r), :] += prev[0, r, x:x + ROWS, half(h)]
                value[h, every(x - base, 6 + r), :] += next_[0, r, x:x + ROWS, half(h)]

    def emit(h, x, result):
        sums[slot, x - low, :, half(h)] += result

    retreat(low, high, value, base, near, velocity, emit, weights, pos_pad, neg_pad, lhs, along)


def call(body, scalars, ins, outs, arrays, scratch, velocity=None, part=(0, SX), nbytes=40_000_000):
    fixed = len(scalars)
    views = [view for view, _ in ins] + [view for _, view in outs]
    low, high = part
    in_specs = [pl.BlockSpec(memory_space=pltpu.SMEM)] * fixed
    in_specs += [pl.BlockSpec(memory_space=space) for _, space in ins]
    if velocity is not None:
        scratch = scratch + [pltpu.VMEM((2, 3, high - low, ROWS, NZ), jnp.int32), pltpu.SemaphoreType.DMA((2,))]
        in_specs += [pl.BlockSpec(memory_space=pltpu.HBM)]
        arrays = arrays + (velocity,)

    def kernel(*refs):
        refs = list(refs)
        more = {}
        if velocity is not None:
            source = refs.pop(fixed + len(ins))
            buffer, sem = refs[-2:]
            refs = refs[:-2]

            def fetch(s, slot):
                return pltpu.make_async_copy(source.at[s, :, pl.ds(low, high - low)], buffer.at[slot], sem.at[slot])

            fetch(0, 0).start()

        def one(s, carry):
            seen = [view(ref, s, refs[0]) for view, ref in zip(views, refs[fixed:])]
            if velocity is not None:
                slot = s % 2

                @pl.when(s + 1 < SUBS)
                def ahead():
                    fetch(s + 1, 1 - slot).start()

                fetch(s, slot).wait()
                more["velocity"] = buffer.at[pl.ds(slot, 1)]
            body(s, *refs[:fixed], *seen, *refs[fixed + len(views):], **more)
            return carry

        lax.fori_loop(0, SUBS, one, 0)

    return pl.pallas_call(
        kernel,
        in_specs=in_specs,
        out_specs=[pl.BlockSpec(memory_space=pltpu.VMEM)] * len(outs),
        out_shape=[jax.ShapeDtypeStruct(shape.shape, shape.dtype) for shape, _ in outs],
        scratch_shapes=scratch,
        compiler_params=pltpu.CompilerParams(vmem_limit_bytes=VMEM if velocity is None else STREAMING),
        cost_estimate=pl.CostEstimate(flops=nbytes, bytes_accessed=nbytes, transcendentals=0),
    )(*scalars, *arrays)


def everything(ref, s, groups):
    return ref


def subject(ref, s, groups):
    return ref.at[pl.ds(s, 1)]


def pair(ref, s, groups):
    return ref.at[:, pl.ds(s, 1)]


def swap(even, odd, count):
    pairs = [[(i, i + 1) for i in range(first, count - 1, 2)] for first in (0, 1)]
    both_ways = [[(a, b) for a, b in part] + [(b, a) for a, b in part] for part in pairs]
    odd = lax.ppermute(odd, "tile", both_ways[1])
    even = lax.ppermute(even, "tile", both_ways[0])
    return even, odd


def shards(template, images, velocity, groups):
    count = lax.axis_size("tile")
    place = lax.axis_index("subj")
    core, high_y = place % 2, place // 2
    some = GROUPS // 2
    core_pairs = [(0, 1), (1, 0), (2, 3), (3, 2)]
    y_pairs = [(0, 2), (2, 0), (1, 3), (3, 1)]
    is_odd = lax.axis_index("tile") % 2 == 1
    side = jnp.stack([core, high_y, is_odd]).astype(jnp.int32)
    plus, minus = stencil(PLUS), stencil(MINUS)
    onward = np.concatenate([plus.T, minus.T], axis=1)
    onward = jnp.asarray(np.concatenate([onward, onward], axis=0), jnp.bfloat16)
    backward = jnp.asarray(np.concatenate([plus, plus, minus, minus], axis=0), jnp.bfloat16)
    f32, bf16 = jnp.float32, jnp.bfloat16
    vmem = lambda shape, dtype=f32: pltpu.VMEM(shape, dtype)
    shape = jax.ShapeDtypeStruct
    field = shape((SUBS, 2, SX * ROWS, HALF), f32)
    edge = shape((SUBS, 2, SX, NZ), f32)
    edges_both = shape((2, SUBS, 2, SX, NZ), f32)
    one, all_ = (subject, pltpu.VMEM), (everything, pltpu.VMEM)
    rows = SX * ROWS

    mine = lax.dynamic_slice_in_dim(template, core * some, some, axis=0)
    ends = jnp.swapaxes(jnp.concatenate([mine[:, :, 0:2], mine[:, :, 6:8]], axis=2), 1, 2)
    up, down = ends[:, 0:2], ends[:, 2:4]
    even_own, odd_own = swap(jnp.where(is_odd, up, down), jnp.where(is_odd, down, up), count)

    moved, sides = call(
        first_kernel,
        (groups,),
        [(lambda ref, s, g: ref.at[pl.ds(g[s], 1)], pltpu.VMEM), all_],
        [(field, subject), (shape((SUBS, 4, SX, NZ), f32), subject)],
        (template, onward),
        [vmem(pad_rows(SX + 4)), vmem((2, rows, HALF)), vmem((rows, 2 * NZ), bf16), vmem((rows, 2 * NZ))],
        velocity=velocity,
    )
    even_own, odd_own, sides = lax.optimization_barrier((even_own, odd_own, sides))
    even_other = lax.ppermute(even_own, "subj", core_pairs)
    odd_other = lax.ppermute(odd_own, "subj", core_pairs)
    of_group = (lambda ref, s, g: ref.at[pl.ds(g[s] % some, 1)], pltpu.VMEM)
    (both,) = call(
        first_border,
        (groups, side),
        [one] + [of_group] * 4 + [one],
        [(edges_both, pair)],
        (moved, even_own, even_other, odd_own, odd_other, sides),
        [],
    )
    even, odd = swap(both[0], both[1], count)
    (residual,) = call(
        second_kernel,
        (groups, side),
        [one, (pair, pltpu.VMEM), one, all_],
        [(field, subject)],
        (moved, both, images, onward),
        [vmem(pad_rows(SX + 4)), vmem((rows, 2 * NZ), bf16), vmem((rows, 2 * NZ))],
        velocity=velocity,
    )
    top, bottom, both = call(
        second_border,
        (groups, side),
        [one] * 4,
        [(edge, subject)] * 2 + [(edges_both, pair)],
        (residual, even, odd, sides),
        [],
    )
    even, odd = swap(both[0], both[1], count)
    (adjoint,) = call(
        third_kernel,
        (groups,),
        [one] * 3 + [all_],
        [(field, subject)],
        (residual, top, bottom, backward),
        [
            vmem((2, rows, HALF)),
            vmem(pad_rows(SX + 8)),
            vmem(pad_rows(SX + 8)),
            vmem((rows, 4 * NZ), bf16),
            vmem((rows, NZ)),
        ],
        velocity=velocity,
    )

    (edges,) = call(
        third_border,
        (groups, side),
        [one] * 4,
        [(shape((GROUPS, 4 * SX, NZ), f32), everything)],
        (adjoint, even, odd, sides),
        [],
    )
    adjoint, edges = lax.optimization_barrier((adjoint, edges))
    edges4 = edges[some:] + lax.ppermute(edges[:some], "subj", core_pairs)

    cuts = (0,) + CUTS + (SX,)
    sums4, sums2 = [], []
    for c, (low, high) in enumerate(zip(cuts, cuts[1:])):
        n = high - low
        span = min(high + 8, SX) - max(low - 8, 0)
        part = (max(low - 2, 0), min(high + 2, SX))
        if c == 1:
            adjoint, sums4[0] = lax.optimization_barrier((adjoint, sums4[0]))
        if c == 2:
            adjoint, ends, sums2[0] = lax.optimization_barrier((adjoint, ends, sums2[0]))
            ends = ends[2:] + lax.ppermute(ends[:2], "subj", y_pairs)
        (sums,) = call(
            functools.partial(fourth_kernel, low, high, part[0]),
            (groups, side),
            [one] * 3 + [all_],
            [(shape((GROUPS, n, ROWS, NZ), f32), everything)],
            (adjoint, even, odd, backward),
            [
                vmem((2, span * ROWS, HALF)),
                vmem(pad_rows(n + 8)),
                vmem(pad_rows(n + 8)),
                vmem((n * ROWS, 4 * NZ), bf16),
                vmem((n * ROWS, NZ)),
            ],
            velocity=velocity,
            part=part,
        )
        adjoint, sums = lax.optimization_barrier((adjoint, sums))
        if c == 0:
            sums, edges4 = lax.optimization_barrier((sums, edges4))
            up, down = edges4[:, :2 * SX], edges4[:, 2 * SX:]
            ends = swap(jnp.where(is_odd, up, down), jnp.where(is_odd, down, up), count)
        if c == 1:
            sums, *ends = lax.optimization_barrier((sums, *ends))
            ends = jnp.concatenate([jnp.where(is_odd, *ends), jnp.where(is_odd, *ends[::-1])], axis=1)
        if c == 2:
            sums, ends = lax.optimization_barrier((sums, ends))
        sums4.append(sums[some:] + lax.ppermute(sums[:some], "subj", core_pairs))
        sums2.append(sums4[c][2:] + lax.ppermute(sums4[c][:2], "subj", y_pairs))
    from_prev, from_next = ends[:, :2 * SX], ends[:, 2 * SX:]
    middle = jnp.zeros((2, SX, ROWS - 4, NZ), f32)
    from_prev, from_next = (jnp.swapaxes(e.reshape(2, 2, SX, NZ), 1, 2) for e in (from_prev, from_next))
    return jnp.concatenate(sums2, axis=1) + jnp.concatenate([from_prev, middle, from_next], axis=2)


def solution(mesh):
    in_specs = (
        P(None, None, "tile", None),
        P("subj", None, "tile", None),
        P("subj", None, None, "tile", None),
        P("subj"),
    )
    out_specs = P("subj", None, "tile", None)
    return jax.shard_map(shards, mesh=mesh, in_specs=in_specs, out_specs=out_specs, check_vma=False)
```

```python
import functools

import jax
import jax.numpy as jnp
import numpy as np
from jax import lax
from jax.experimental import pallas as pl
from jax.experimental.pallas import tpu as pltpu
from jax.sharding import PartitionSpec as P

SCALE = 1.0 / (6.0 * 8192.0)
SX = 64
ROWS = 8
NZ = 256
HALF = 128
SUBS = 8
GROUPS = 8
VMEM = 2 * 1024 * 1024
STREAMING = 40 * 1024 * 1024
UNROLL = 4
STRIDE = 16
PLUS = {-2: 1.0, -1: -6.0, 0: 3.0, 1: 2.0}
MINUS = {-1: -2.0, 0: -3.0, 1: 6.0, 2: -1.0}


def padded(n):
    return (n + 7) // 8 * 8


def stencil(taps):
    matrix = np.zeros((NZ, NZ), np.float32)
    for shift, weight in taps.items():
        matrix += weight * np.eye(NZ, k=shift, dtype=np.float32)
    return matrix


def half(h):
    return slice(h * HALF, (h + 1) * HALF)


def eights(start):
    return pl.ds(start if isinstance(start, int) else pl.multiple_of(start, ROWS), ROWS)


def loop(count, body, step=UNROLL, first=0):
    for k in range(first):
        body(k)
    whole = (count - first) // step

    def several(block, carry):
        for k in range(step):
            body(first + block * step + k)
        return carry

    if whole > 0:
        lax.fori_loop(0, whole, several, 0)
    for k in range(first + whole * step, count):
        body(k)


class Padded:
    def __init__(self, ref, low):
        self.ref, self.low = ref, low

    def start(self, x):
        return (x - self.low) * STRIDE + ROWS

    def read(self, h, x, shift=0):
        start = self.start(x)
        return self.ref[h, eights(start) if shift == 0 else pl.ds(start + shift, ROWS), :]

    def write(self, h, x, value):
        self.ref[h, eights(self.start(x)), :] = value

    def every(self, x, row):
        return pl.ds(self.start(x) + row, ROWS, stride=STRIDE)


def pad_rows(slices):
    return (2, slices * STRIDE + 2 * ROWS, HALF)


def upwind(speed, back2, back1, mid3, fore1, fore2):
    speed = speed.astype(jnp.float32)
    forward = speed > 0.0
    near = jnp.where(forward, back1, fore1)
    far = jnp.where(forward, back2, fore2)
    ahead = jnp.where(forward, fore1, back1)
    return jnp.abs(speed) * (far - 6.0 * near + mid3 + (ahead + ahead))


def split(value):
    high = value.astype(jnp.bfloat16)
    return high, (value - high.astype(jnp.float32)).astype(jnp.bfloat16)


def fill(field, ref):
    def body(x):
        for h in range(2):
            field.write(h, x, ref[0, x, :, half(h)])

    loop(SX, body)


def clear(ref):
    ref[...] = jnp.zeros_like(ref)


def every(x, row):
    return pl.ds(x * ROWS + row, ROWS, stride=ROWS)


def of(x):
    return eights(x * ROWS)


def put_rows(dst, top, bottom, low, high, base):
    for x in range(low, high, ROWS):
        for h in range(2):
            for r in range(2):
                dst[h, every(x - base, r), :] = top[0, r, x:x + ROWS, half(h)]
                dst[h, every(x - base, 6 + r), :] = bottom[0, r, x:x + ROWS, half(h)]


def advance(field, velocity, weights, lhs, along, emit):
    def halves(k):
        x = k * 2
        for h in range(2):
            pair = jnp.concatenate([field.read(h, x), field.read(h, x + 1)], axis=0)
            high, rest = split(pair)
            rows = pl.ds(k * 16 if isinstance(k, int) else pl.multiple_of(k * 16, 16), 16)
            lhs[rows, half(h)] = high
            lhs[rows, half(2 + h)] = rest

    loop(SX // 2, halves, UNROLL // 2)
    along[...] = jnp.dot(lhs[...], weights[...], preferred_element_type=jnp.float32)

    def body(x):
        for h in range(2):
            mid = field.read(h, x)
            mid3 = 3.0 * mid
            speed = [velocity[0, d, x, :, half(h)] for d in range(3)]
            change = upwind(speed[0], *(field.read(h, x + s) if s else mid3 for s in (-2, -1, 0, 1, 2)))
            change += upwind(speed[1], *(field.read(h, x, s) if s else mid3 for s in (-2, -1, 0, 1, 2)))
            ahead = speed[2].astype(jnp.float32)
            plus, minus = along[of(x), half(h)], along[of(x), half(2 + h)]
            change += ahead * jnp.where(ahead > 0.0, plus, minus)
            emit(h, x, mid - SCALE * change, speed)

    loop(SX, body)


def first_kernel(s, groups, template, weights, moved, sides, pad, speeds, lhs, along, velocity):
    @pl.when(s == 0)
    def start():
        clear(pad)

    field = Padded(pad, -2)
    fill(field, template)

    def emit(h, x, value, speed):
        moved[0, h, of(x), :] = value
        speeds[h, of(x), :] = speed[1].astype(jnp.float32)

    advance(field, velocity, weights, lhs, along, emit)
    for x in range(0, SX, ROWS):
        for h in range(2):
            for i, r in enumerate((0, 1, 6, 7)):
                sides[0, i, x:x + ROWS, half(h)] = speeds[h, every(x, r), :]


def entering(value, speed, prev, next_, k, h):
    group = slice(k, k + ROWS)
    back2, back1 = prev[0, 0, group, half(h)], prev[0, 1, group, half(h)]
    fore1, fore2 = next_[0, 0, group, half(h)], next_[0, 1, group, half(h)]
    v0, v1, v6, v7 = (speed[0, i, group, half(h)] for i in range(4))
    change = (
        jnp.abs(v0) * jnp.where(v0 > 0.0, back2 - 6.0 * back1, 2.0 * back1),
        jnp.maximum(v1, 0.0) * back1,
        jnp.maximum(-v6, 0.0) * fore1,
        jnp.abs(v7) * jnp.where(v7 > 0.0, 2.0 * fore1, fore2 - 6.0 * fore1),
    )
    return [value[0, h, every(k, r), :] - SCALE * c for r, c in zip((0, 1, 6, 7), change)]


class Picked:
    def __init__(self, yes, first, second):
        self.yes, self.first, self.second = yes, first, second

    def __getitem__(self, index):
        return jnp.where(self.yes, self.first[index], self.second[index])


def arrivals(side, even, odd):
    yes = side[2] == 1
    return Picked(yes, even, odd), Picked(yes, odd, even)


def departures(side, both):
    return both.at[1 - side[2]], both.at[side[2]]


def first_border(s, groups, side, moved, even_own, even_other, odd_own, odd_other, sides, both):
    own = (groups[s] // (GROUPS // 2)) == side[0]
    up, down = departures(side, both)

    def finish(even, odd):
        prev, next_ = arrivals(side, even, odd)
        for k in range(0, SX, ROWS):
            for h in range(2):
                rows = entering(moved, sides, prev, next_, k, h)
                for r in range(2):
                    up[0, r, k:k + ROWS, half(h)] = rows[r]
                    down[0, r, k:k + ROWS, half(h)] = rows[2 + r]

    @pl.when(own)
    def from_own():
        finish(even_own, odd_own)

    @pl.when(jnp.logical_not(own))
    def from_other():
        finish(even_other, odd_other)


def second_kernel(s, groups, side, moved, both, images, weights, residual, pad, lhs, along, velocity):
    @pl.when(s == 0)
    def start():
        clear(pad)

    field = Padded(pad, -2)
    up, down = departures(side, both)

    def copy(x):
        for h in range(2):
            field.write(h, x, moved[0, h, of(x), :])

    loop(SX, copy)
    for x in range(0, SX, ROWS):
        for h in range(2):
            for r in range(2):
                pad[h, field.every(x, r), :] = up[0, r, x:x + ROWS, half(h)]
                pad[h, field.every(x, 6 + r), :] = down[0, r, x:x + ROWS, half(h)]

    def emit(h, x, value, speed):
        residual[0, h, of(x), :] = value - images[0, x, :, half(h)]

    advance(field, velocity, weights, lhs, along, emit)


def second_border(s, groups, side, residual, even, odd, sides, top, bottom, both):
    prev, next_ = arrivals(side, even, odd)
    up, down = departures(side, both)
    for k in range(0, SX, ROWS):
        group = slice(k, k + ROWS)
        for h in range(2):
            rows = dict(zip((0, 1, 6, 7), entering(residual, sides, prev, next_, k, h)))
            speed = dict(zip((0, 1, 6, 7), (sides[0, i, group, half(h)] for i in range(4))))
            for r in range(2):
                top[0, r, group, half(h)] = rows[r]
                bottom[0, r, group, half(h)] = rows[6 + r]
            pos = {r: jnp.maximum(speed[r], 0.0) * rows[r] for r in (0, 1, 7)}
            neg = {r: jnp.minimum(speed[r], 0.0) * rows[r] for r in (0, 6, 7)}
            for ref, r, change in outgoing(pos, neg):
                (up, down)[ref][0, r, group, half(h)] = change


def outgoing(pos, neg):
    return (
        (0, 0, -SCALE * pos[0]),
        (0, 1, -SCALE * (pos[1] - 6.0 * pos[0] - 2.0 * neg[0])),
        (1, 0, -SCALE * (2.0 * pos[7] + 6.0 * neg[7] - neg[6])),
        (1, 1, SCALE * neg[7]),
    )


def retreat(low, high, value, base, near, velocity, emit, weights, pos_pad, neg_pad, lhs, along):
    def get(h, x):
        return value[h, of(x - base), :]

    def speed_of(d, h, x):
        return velocity[0, d, x - near, :, half(h)]

    n = high - low
    pos_field, neg_field = Padded(pos_pad, low), Padded(neg_pad, low)

    def before(k):
        x = low + k * 2
        rows = pl.ds(k * 16 if isinstance(k, int) else pl.multiple_of(k * 16, 16), 16)
        for h in range(2):
            pairs = []
            for i in range(2):
                here = get(h, x + i)
                speed = speed_of(1, h, x + i).astype(jnp.float32)
                pos_field.write(h, x + i, jnp.maximum(speed, 0.0) * here)
                neg_field.write(h, x + i, jnp.minimum(speed, 0.0) * here)
                speed = speed_of(2, h, x + i).astype(jnp.float32)
                pairs.append((jnp.maximum(speed, 0.0) * here, jnp.minimum(speed, 0.0) * here))
            for j in range(2):
                top, rest = split(jnp.concatenate([pairs[0][j], pairs[1][j]], axis=0))
                lhs[rows, half(4 * j + h)] = top
                lhs[rows, half(4 * j + 2 + h)] = rest

    loop(n // 2, before, UNROLL // 2)
    along[...] = jnp.dot(lhs[...], weights[...], preferred_element_type=jnp.float32)

    def one(h, x, carry, inside):
        now0, now1, now2, now3 = carry
        here = get(h, x)
        twice = here + here
        speed = speed_of(0, h, x).astype(jnp.float32)
        pos, neg = jnp.maximum(speed, 0.0) * twice, jnp.minimum(speed, 0.0) * twice
        if not isinstance(x, int) or x >= low + 2:
            emit(h, x - 2, get(h, x - 2) - SCALE * (now0 + 0.5 * pos))
        if inside:
            ypos, yneg = pos_field.read(h, x), neg_field.read(h, x)
            own = pos_field.read(h, x, 2) - neg_field.read(h, x, -2)
            own += 2.0 * (pos_field.read(h, x, -1) - neg_field.read(h, x, 1))
            own -= 6.0 * (pos_field.read(h, x, 1) - neg_field.read(h, x, -1))
            own += 3.0 * (ypos - yneg) + 1.5 * (pos - neg)
            own += along[eights((x - low) * ROWS), half(h)]
            now2 = now2 + own
        return now1 - (3.0 * pos + neg), now2, now3 + (pos + 3.0 * neg), -0.5 * neg

    def body(x, carry, inside=True):
        return tuple(one(h, x, carry[h], inside) for h in range(2))

    zero = jnp.zeros((ROWS, HALF), jnp.float32)
    carry = ((zero,) * 4,) * 2
    first, last = low + 2, high
    for x in range(max(low - 2, 0), first):
        carry = body(x, carry, low <= x)
    whole = (last - first) // UNROLL

    def several(block, carry):
        for k in range(UNROLL):
            carry = body(first + block * UNROLL + k, carry)
        return carry

    carry = lax.fori_loop(0, whole, several, carry)
    for x in range(first + whole * UNROLL, last):
        carry = body(x, carry)
    for x in range(last, min(high + 2, SX)):
        carry = body(x, carry, False)
    if high == SX:
        for h in range(2):
            emit(h, SX - 2, get(h, SX - 2) - SCALE * carry[h][0])
            emit(h, SX - 1, get(h, SX - 1) - SCALE * carry[h][1])


def third_kernel(s, groups, residual, top, bottom, weights, adjoint, value, pos_pad, neg_pad, lhs, along, velocity):
    @pl.when(s == 0)
    def start():
        clear(pos_pad)
        clear(neg_pad)

    def copy(x):
        for h in range(2):
            value[h, of(x), :] = residual[0, h, of(x), :]

    loop(SX, copy)
    put_rows(value, top, bottom, 0, SX, 0)

    def emit(h, x, result):
        adjoint[0, h, of(x), :] = result

    retreat(0, SX, value, 0, 0, velocity, emit, weights, pos_pad, neg_pad, lhs, along)


def slot_of(group, side):
    owner = group // 2
    core = (owner % 2 == side[0]).astype(jnp.int32)
    return core * 4 + (owner // 2 == side[1]).astype(jnp.int32) * 2 + group % 2


def third_border(s, groups, side, adjoint, even, odd, sides, edges):
    prev, next_ = arrivals(side, even, odd)
    slot = slot_of(groups[s], side)

    @pl.when(s == 0)
    def start():
        clear(edges)

    for k in range(0, SX, ROWS):
        group = slice(k, k + ROWS)
        for h in range(2):
            value = {r: adjoint[0, h, every(k, r), :] + prev[0, r, group, half(h)] for r in (0, 1)}
            value.update({6 + r: adjoint[0, h, every(k, 6 + r), :] + next_[0, r, group, half(h)] for r in (0, 1)})
            speed = dict(zip((0, 1, 6, 7), (sides[0, i, group, half(h)] for i in range(4))))
            pos = {r: jnp.maximum(speed[r], 0.0) * value[r] for r in (0, 1, 7)}
            neg = {r: jnp.minimum(speed[r], 0.0) * value[r] for r in (0, 6, 7)}
            for ref, r, change in outgoing(pos, neg):
                at = (2 * ref + r) * SX + k
                edges[slot, at:at + ROWS, half(h)] += change


def fourth_kernel(low, high, near, s, groups, side, adjoint, even, odd, weights, sums,
                  value, pos_pad, neg_pad, lhs, along, velocity):
    prev, next_ = arrivals(side, even, odd)
    slot = slot_of(groups[s], side)

    @pl.when(s == 0)
    def start():
        for ref in (sums, pos_pad, neg_pad):
            clear(ref)

    base, stop = max(low - 8, 0), min(high + 8, SX)

    def copy(k):
        for h in range(2):
            value[h, of(k), :] = adjoint[0, h, of(base + k), :]

    loop(stop - base, copy)
    for x in range(base, stop, ROWS):
        for h in range(2):
            for r in range(2):
                value[h, every(x - base, r), :] += prev[0, r, x:x + ROWS, half(h)]
                value[h, every(x - base, 6 + r), :] += next_[0, r, x:x + ROWS, half(h)]

    def emit(h, x, result):
        sums[slot, x - low, :, half(h)] += result

    retreat(low, high, value, base, near, velocity, emit, weights, pos_pad, neg_pad, lhs, along)


def call(body, scalars, ins, outs, arrays, scratch, velocity=None, part=(0, SX), nbytes=40_000_000):
    fixed = len(scalars)
    views = [view for view, _ in ins] + [view for _, view in outs]
    low, high = part
    in_specs = [pl.BlockSpec(memory_space=pltpu.SMEM)] * fixed
    in_specs += [pl.BlockSpec(memory_space=space) for _, space in ins]
    if velocity is not None:
        scratch = scratch + [pltpu.VMEM((2, 3, high - low, ROWS, NZ), jnp.int32), pltpu.SemaphoreType.DMA((2,))]
        in_specs += [pl.BlockSpec(memory_space=pltpu.HBM)]
        arrays = arrays + (velocity,)

    def kernel(*refs):
        refs = list(refs)
        more = {}
        if velocity is not None:
            source = refs.pop(fixed + len(ins))
            buffer, sem = refs[-2:]
            refs = refs[:-2]

            def fetch(s, slot):
                return pltpu.make_async_copy(source.at[s, :, pl.ds(low, high - low)], buffer.at[slot], sem.at[slot])

            fetch(0, 0).start()

        def one(s, carry):
            seen = [view(ref, s, refs[0]) for view, ref in zip(views, refs[fixed:])]
            if velocity is not None:
                slot = s % 2

                @pl.when(s + 1 < SUBS)
                def ahead():
                    fetch(s + 1, 1 - slot).start()

                fetch(s, slot).wait()
                more["velocity"] = buffer.at[pl.ds(slot, 1)]
            body(s, *refs[:fixed], *seen, *refs[fixed + len(views):], **more)
            return carry

        lax.fori_loop(0, SUBS, one, 0)

    return pl.pallas_call(
        kernel,
        in_specs=in_specs,
        out_specs=[pl.BlockSpec(memory_space=pltpu.VMEM)] * len(outs),
        out_shape=[jax.ShapeDtypeStruct(shape.shape, shape.dtype) for shape, _ in outs],
        scratch_shapes=scratch,
        compiler_params=pltpu.CompilerParams(vmem_limit_bytes=VMEM if velocity is None else STREAMING),
        cost_estimate=pl.CostEstimate(flops=nbytes, bytes_accessed=nbytes, transcendentals=0),
    )(*scalars, *arrays)


def everything(ref, s, groups):
    return ref


def subject(ref, s, groups):
    return ref.at[pl.ds(s, 1)]


def pair(ref, s, groups):
    return ref.at[:, pl.ds(s, 1)]


def swap(even, odd, count):
    pairs = [[(i, i + 1) for i in range(first, count - 1, 2)] for first in (0, 1)]
    both_ways = [[(a, b) for a, b in part] + [(b, a) for a, b in part] for part in pairs]
    odd = lax.ppermute(odd, "tile", both_ways[1])
    even = lax.ppermute(even, "tile", both_ways[0])
    return even, odd


def shards(template, images, velocity, groups):
    count = lax.axis_size("tile")
    place = lax.axis_index("subj")
    core, high_y = place % 2, place // 2
    some = GROUPS // 2
    core_pairs = [(0, 1), (1, 0), (2, 3), (3, 2)]
    y_pairs = [(0, 2), (2, 0), (1, 3), (3, 1)]
    is_odd = lax.axis_index("tile") % 2 == 1
    side = jnp.stack([core, high_y, is_odd]).astype(jnp.int32)
    plus, minus = stencil(PLUS), stencil(MINUS)
    onward = np.concatenate([plus.T, minus.T], axis=1)
    onward = jnp.asarray(np.concatenate([onward, onward], axis=0), jnp.bfloat16)
    backward = jnp.asarray(np.concatenate([plus, plus, minus, minus], axis=0), jnp.bfloat16)
    f32, bf16 = jnp.float32, jnp.bfloat16
    vmem = lambda shape, dtype=f32: pltpu.VMEM(shape, dtype)
    shape = jax.ShapeDtypeStruct
    field = shape((SUBS, 2, SX * ROWS, HALF), f32)
    edge = shape((SUBS, 2, SX, NZ), f32)
    edges_both = shape((2, SUBS, 2, SX, NZ), f32)
    one, all_ = (subject, pltpu.VMEM), (everything, pltpu.VMEM)
    rows = SX * ROWS

    mine = lax.dynamic_slice_in_dim(template, core * some, some, axis=0)
    ends = jnp.swapaxes(jnp.concatenate([mine[:, :, 0:2], mine[:, :, 6:8]], axis=2), 1, 2)
    up, down = ends[:, 0:2], ends[:, 2:4]
    even_own, odd_own = swap(jnp.where(is_odd, up, down), jnp.where(is_odd, down, up), count)

    moved, sides = call(
        first_kernel,
        (groups,),
        [(lambda ref, s, g: ref.at[pl.ds(g[s], 1)], pltpu.VMEM), all_],
        [(field, subject), (shape((SUBS, 4, SX, NZ), f32), subject)],
        (template, onward),
        [vmem(pad_rows(SX + 4)), vmem((2, rows, HALF)), vmem((rows, 2 * NZ), bf16), vmem((rows, 2 * NZ))],
        velocity=velocity,
    )
    even_own, odd_own, sides = lax.optimization_barrier((even_own, odd_own, sides))
    even_other = lax.ppermute(even_own, "subj", core_pairs)
    odd_other = lax.ppermute(odd_own, "subj", core_pairs)
    of_group = (lambda ref, s, g: ref.at[pl.ds(g[s] % some, 1)], pltpu.VMEM)
    (both,) = call(
        first_border,
        (groups, side),
        [one] + [of_group] * 4 + [one],
        [(edges_both, pair)],
        (moved, even_own, even_other, odd_own, odd_other, sides),
        [],
    )
    even, odd = swap(both[0], both[1], count)
    (residual,) = call(
        second_kernel,
        (groups, side),
        [one, (pair, pltpu.VMEM), one, all_],
        [(field, subject)],
        (moved, both, images, onward),
        [vmem(pad_rows(SX + 4)), vmem((rows, 2 * NZ), bf16), vmem((rows, 2 * NZ))],
        velocity=velocity,
    )
    top, bottom, both = call(
        second_border,
        (groups, side),
        [one] * 4,
        [(edge, subject)] * 2 + [(edges_both, pair)],
        (residual, even, odd, sides),
        [],
    )
    even, odd = swap(both[0], both[1], count)
    (adjoint,) = call(
        third_kernel,
        (groups,),
        [one] * 3 + [all_],
        [(field, subject)],
        (residual, top, bottom, backward),
        [
            vmem((2, rows, HALF)),
            vmem(pad_rows(SX + 8)),
            vmem(pad_rows(SX + 8)),
            vmem((rows, 4 * NZ), bf16),
            vmem((rows, NZ)),
        ],
        velocity=velocity,
    )

    (edges,) = call(
        third_border,
        (groups, side),
        [one] * 4,
        [(shape((GROUPS, 4 * SX, NZ), f32), everything)],
        (adjoint, even, odd, sides),
        [],
    )
    edges4 = edges[some:] + lax.ppermute(edges[:some], "subj", core_pairs)
    adjoint, edges4 = lax.optimization_barrier((adjoint, edges4))
    up, down = edges4[:, :2 * SX], edges4[:, 2 * SX:]
    even_ends, odd_ends = swap(jnp.where(is_odd, up, down), jnp.where(is_odd, down, up), count)
    (sums,) = call(
        functools.partial(fourth_kernel, 0, SX, 0),
        (groups, side),
        [one] * 3 + [all_],
        [(shape((GROUPS, SX, ROWS, NZ), f32), everything)],
        (adjoint, even, odd, backward),
        [
            vmem((2, rows, HALF)),
            vmem(pad_rows(SX + 8)),
            vmem(pad_rows(SX + 8)),
            vmem((rows, 4 * NZ), bf16),
            vmem((rows, NZ)),
        ],
        velocity=velocity,
    )
    sums, even_ends, odd_ends = lax.optimization_barrier((sums, even_ends, odd_ends))
    arrived = lax.ppermute(sums[:some], "subj", core_pairs)
    middle = jnp.zeros((some, SX, ROWS - 4, NZ), f32)
    from_prev, from_next = jnp.where(is_odd, even_ends, odd_ends), jnp.where(is_odd, odd_ends, even_ends)
    from_prev, from_next = (jnp.swapaxes(e.reshape(some, 2, SX, NZ), 1, 2) for e in (from_prev, from_next))
    sums4 = sums[some:] + jnp.concatenate([from_prev, middle, from_next], axis=2)
    sums4 = sums4 + arrived
    return sums4[2:] + lax.ppermute(sums4[:2], "subj", y_pairs)


def solution(mesh):
    in_specs = (
        P(None, None, "tile", None),
        P("subj", None, "tile", None),
        P("subj", None, None, "tile", None),
        P("subj"),
    )
    out_specs = P("subj", None, "tile", None)
    return jax.shard_map(shards, mesh=mesh, in_specs=in_specs, out_specs=out_specs, check_vma=False)
```

```python
import functools

import jax
import jax.numpy as jnp
import numpy as np
from jax import lax
from jax.experimental import pallas as pl
from jax.experimental.pallas import tpu as pltpu
from jax.sharding import PartitionSpec as P

SCALE = 1.0 / (6.0 * 8192.0)
SX = 64
ROWS = 8
NZ = 256
HALF = 128
SUBS = 8
GROUPS = 8
VMEM = 2 * 1024 * 1024
STREAMING = 40 * 1024 * 1024
UNROLL = 8
STRIDE = 16
PLUS = {-2: 1.0, -1: -6.0, 0: 3.0, 1: 2.0}
MINUS = {-1: -2.0, 0: -3.0, 1: 6.0, 2: -1.0}


def padded(n):
    return (n + 7) // 8 * 8


def stencil(taps):
    matrix = np.zeros((NZ, NZ), np.float32)
    for shift, weight in taps.items():
        matrix += weight * np.eye(NZ, k=shift, dtype=np.float32)
    return matrix


def half(h):
    return slice(h * HALF, (h + 1) * HALF)


def eights(start):
    return pl.ds(start if isinstance(start, int) else pl.multiple_of(start, ROWS), ROWS)


def loop(count, body, step=UNROLL, first=0):
    for k in range(first):
        body(k)
    whole = (count - first) // step

    def several(block, carry):
        for k in range(step):
            body(first + block * step + k)
        return carry

    if whole > 0:
        lax.fori_loop(0, whole, several, 0)
    for k in range(first + whole * step, count):
        body(k)


class Padded:
    def __init__(self, ref, low):
        self.ref, self.low = ref, low

    def start(self, x):
        return (x - self.low) * STRIDE + ROWS

    def read(self, h, x, shift=0):
        start = self.start(x)
        return self.ref[h, eights(start) if shift == 0 else pl.ds(start + shift, ROWS), :]

    def write(self, h, x, value):
        self.ref[h, eights(self.start(x)), :] = value

    def every(self, x, row):
        return pl.ds(self.start(x) + row, ROWS, stride=STRIDE)


def pad_rows(slices):
    return (2, slices * STRIDE + 2 * ROWS, HALF)


def upwind(speed, back2, back1, mid3, fore1, fore2):
    speed = speed.astype(jnp.float32)
    forward = speed > 0.0
    near = jnp.where(forward, back1, fore1)
    far = jnp.where(forward, back2, fore2)
    ahead = jnp.where(forward, fore1, back1)
    return jnp.abs(speed) * (far - 6.0 * near + mid3 + (ahead + ahead))


def split(value):
    high = value.astype(jnp.bfloat16)
    return high, (value - high.astype(jnp.float32)).astype(jnp.bfloat16)


def fill(field, ref):
    def body(x):
        for h in range(2):
            field.write(h, x, ref[0, x, :, half(h)])

    loop(SX, body)


def clear(ref):
    ref[...] = jnp.zeros_like(ref)


def every(x, row):
    return pl.ds(x * ROWS + row, ROWS, stride=ROWS)


def of(x):
    return eights(x * ROWS)


def put_rows(dst, top, bottom, low, high, base):
    for x in range(low, high, ROWS):
        for h in range(2):
            for r in range(2):
                dst[h, every(x - base, r), :] = top[0, r, x:x + ROWS, half(h)]
                dst[h, every(x - base, 6 + r), :] = bottom[0, r, x:x + ROWS, half(h)]


def advance(field, velocity, weights, lhs, along, emit):
    def halves(k):
        x = k * 2
        for h in range(2):
            pair = jnp.concatenate([field.read(h, x), field.read(h, x + 1)], axis=0)
            high, rest = split(pair)
            rows = pl.ds(k * 16 if isinstance(k, int) else pl.multiple_of(k * 16, 16), 16)
            lhs[rows, half(h)] = high
            lhs[rows, half(2 + h)] = rest

    loop(SX // 2, halves, UNROLL // 2)
    along[...] = jnp.dot(lhs[...], weights[...], preferred_element_type=jnp.float32)

    def body(x):
        for h in range(2):
            mid = field.read(h, x)
            mid3 = 3.0 * mid
            speed = [velocity[0, d, x, :, half(h)] for d in range(3)]
            change = upwind(speed[0], *(field.read(h, x + s) if s else mid3 for s in (-2, -1, 0, 1, 2)))
            change += upwind(speed[1], *(field.read(h, x, s) if s else mid3 for s in (-2, -1, 0, 1, 2)))
            ahead = speed[2].astype(jnp.float32)
            plus, minus = along[of(x), half(h)], along[of(x), half(2 + h)]
            change += ahead * jnp.where(ahead > 0.0, plus, minus)
            emit(h, x, mid - SCALE * change, speed)

    loop(SX, body)


def first_kernel(s, groups, template, weights, moved, sides, pad, speeds, lhs, along, velocity):
    @pl.when(s == 0)
    def start():
        clear(pad)

    field = Padded(pad, -2)
    fill(field, template)

    def emit(h, x, value, speed):
        moved[0, h, of(x), :] = value
        speeds[h, of(x), :] = speed[1].astype(jnp.float32)

    advance(field, velocity, weights, lhs, along, emit)
    for x in range(0, SX, ROWS):
        for h in range(2):
            for i, r in enumerate((0, 1, 6, 7)):
                sides[0, i, x:x + ROWS, half(h)] = speeds[h, every(x, r), :]


def entering(value, speed, prev, next_, k, h):
    group = slice(k, k + ROWS)
    back2, back1 = prev[0, 0, group, half(h)], prev[0, 1, group, half(h)]
    fore1, fore2 = next_[0, 0, group, half(h)], next_[0, 1, group, half(h)]
    v0, v1, v6, v7 = (speed[0, i, group, half(h)] for i in range(4))
    change = (
        jnp.abs(v0) * jnp.where(v0 > 0.0, back2 - 6.0 * back1, 2.0 * back1),
        jnp.maximum(v1, 0.0) * back1,
        jnp.maximum(-v6, 0.0) * fore1,
        jnp.abs(v7) * jnp.where(v7 > 0.0, 2.0 * fore1, fore2 - 6.0 * fore1),
    )
    return [value[0, h, every(k, r), :] - SCALE * c for r, c in zip((0, 1, 6, 7), change)]


class Picked:
    def __init__(self, yes, first, second):
        self.yes, self.first, self.second = yes, first, second

    def __getitem__(self, index):
        return jnp.where(self.yes, self.first[index], self.second[index])


def arrivals(side, even, odd):
    yes = side[2] == 1
    return Picked(yes, even, odd), Picked(yes, odd, even)


def departures(side, both):
    return both.at[1 - side[2]], both.at[side[2]]


def first_border(s, groups, side, moved, even_own, even_other, odd_own, odd_other, sides, both):
    own = (groups[s] // (GROUPS // 2)) == side[0]
    up, down = departures(side, both)

    def finish(even, odd):
        prev, next_ = arrivals(side, even, odd)
        for k in range(0, SX, ROWS):
            for h in range(2):
                rows = entering(moved, sides, prev, next_, k, h)
                for r in range(2):
                    up[0, r, k:k + ROWS, half(h)] = rows[r]
                    down[0, r, k:k + ROWS, half(h)] = rows[2 + r]

    @pl.when(own)
    def from_own():
        finish(even_own, odd_own)

    @pl.when(jnp.logical_not(own))
    def from_other():
        finish(even_other, odd_other)


def second_kernel(s, groups, side, moved, both, images, weights, residual, pad, lhs, along, velocity):
    @pl.when(s == 0)
    def start():
        clear(pad)

    field = Padded(pad, -2)
    up, down = departures(side, both)

    def copy(x):
        for h in range(2):
            field.write(h, x, moved[0, h, of(x), :])

    loop(SX, copy)
    for x in range(0, SX, ROWS):
        for h in range(2):
            for r in range(2):
                pad[h, field.every(x, r), :] = up[0, r, x:x + ROWS, half(h)]
                pad[h, field.every(x, 6 + r), :] = down[0, r, x:x + ROWS, half(h)]

    def emit(h, x, value, speed):
        residual[0, h, of(x), :] = value - images[0, x, :, half(h)]

    advance(field, velocity, weights, lhs, along, emit)


def second_border(s, groups, side, residual, even, odd, sides, top, bottom, both):
    prev, next_ = arrivals(side, even, odd)
    up, down = departures(side, both)
    for k in range(0, SX, ROWS):
        group = slice(k, k + ROWS)
        for h in range(2):
            rows = dict(zip((0, 1, 6, 7), entering(residual, sides, prev, next_, k, h)))
            speed = dict(zip((0, 1, 6, 7), (sides[0, i, group, half(h)] for i in range(4))))
            for r in range(2):
                top[0, r, group, half(h)] = rows[r]
                bottom[0, r, group, half(h)] = rows[6 + r]
            pos = {r: jnp.maximum(speed[r], 0.0) * rows[r] for r in (0, 1, 7)}
            neg = {r: jnp.minimum(speed[r], 0.0) * rows[r] for r in (0, 6, 7)}
            for ref, r, change in outgoing(pos, neg):
                (up, down)[ref][0, r, group, half(h)] = change


def outgoing(pos, neg):
    return (
        (0, 0, -SCALE * pos[0]),
        (0, 1, -SCALE * (pos[1] - 6.0 * pos[0] - 2.0 * neg[0])),
        (1, 0, -SCALE * (2.0 * pos[7] + 6.0 * neg[7] - neg[6])),
        (1, 1, SCALE * neg[7]),
    )


def retreat(low, high, value, base, near, velocity, emit, weights, pos_pad, neg_pad, lhs, along):
    def get(h, x):
        return value[h, of(x - base), :]

    def speed_of(d, h, x):
        return velocity[0, d, x - near, :, half(h)]

    n = high - low
    pos_field, neg_field = Padded(pos_pad, low), Padded(neg_pad, low)

    def before(k):
        x = low + k * 2
        rows = pl.ds(k * 16 if isinstance(k, int) else pl.multiple_of(k * 16, 16), 16)
        for h in range(2):
            pairs = []
            for i in range(2):
                here = get(h, x + i)
                speed = speed_of(1, h, x + i).astype(jnp.float32)
                pos_field.write(h, x + i, jnp.maximum(speed, 0.0) * here)
                neg_field.write(h, x + i, jnp.minimum(speed, 0.0) * here)
                speed = speed_of(2, h, x + i).astype(jnp.float32)
                pairs.append((jnp.maximum(speed, 0.0) * here, jnp.minimum(speed, 0.0) * here))
            for j in range(2):
                top, rest = split(jnp.concatenate([pairs[0][j], pairs[1][j]], axis=0))
                lhs[rows, half(4 * j + h)] = top
                lhs[rows, half(4 * j + 2 + h)] = rest

    loop(n // 2, before, UNROLL // 2)
    along[...] = jnp.dot(lhs[...], weights[...], preferred_element_type=jnp.float32)

    def one(h, x, carry, inside):
        now0, now1, now2, now3 = carry
        here = get(h, x)
        twice = here + here
        speed = speed_of(0, h, x).astype(jnp.float32)
        pos, neg = jnp.maximum(speed, 0.0) * twice, jnp.minimum(speed, 0.0) * twice
        if not isinstance(x, int) or x >= low + 2:
            emit(h, x - 2, get(h, x - 2) - SCALE * (now0 + 0.5 * pos))
        if inside:
            ypos, yneg = pos_field.read(h, x), neg_field.read(h, x)
            own = pos_field.read(h, x, 2) - neg_field.read(h, x, -2)
            own += 2.0 * (pos_field.read(h, x, -1) - neg_field.read(h, x, 1))
            own -= 6.0 * (pos_field.read(h, x, 1) - neg_field.read(h, x, -1))
            own += 3.0 * (ypos - yneg) + 1.5 * (pos - neg)
            own += along[eights((x - low) * ROWS), half(h)]
            now2 = now2 + own
        return now1 - (3.0 * pos + neg), now2, now3 + (pos + 3.0 * neg), -0.5 * neg

    def body(x, carry, inside=True):
        return tuple(one(h, x, carry[h], inside) for h in range(2))

    zero = jnp.zeros((ROWS, HALF), jnp.float32)
    carry = ((zero,) * 4,) * 2
    first, last = low + 2, high
    for x in range(max(low - 2, 0), first):
        carry = body(x, carry, low <= x)
    whole = (last - first) // UNROLL

    def several(block, carry):
        for k in range(UNROLL):
            carry = body(first + block * UNROLL + k, carry)
        return carry

    carry = lax.fori_loop(0, whole, several, carry)
    for x in range(first + whole * UNROLL, last):
        carry = body(x, carry)
    for x in range(last, min(high + 2, SX)):
        carry = body(x, carry, False)
    if high == SX:
        for h in range(2):
            emit(h, SX - 2, get(h, SX - 2) - SCALE * carry[h][0])
            emit(h, SX - 1, get(h, SX - 1) - SCALE * carry[h][1])


def third_kernel(s, groups, residual, top, bottom, weights, adjoint, value, pos_pad, neg_pad, lhs, along, velocity):
    @pl.when(s == 0)
    def start():
        clear(pos_pad)
        clear(neg_pad)

    def copy(x):
        for h in range(2):
            value[h, of(x), :] = residual[0, h, of(x), :]

    loop(SX, copy)
    put_rows(value, top, bottom, 0, SX, 0)

    def emit(h, x, result):
        adjoint[0, h, of(x), :] = result

    retreat(0, SX, value, 0, 0, velocity, emit, weights, pos_pad, neg_pad, lhs, along)


def slot_of(group, side):
    owner = group // 2
    core = (owner % 2 == side[0]).astype(jnp.int32)
    return core * 4 + (owner // 2 == side[1]).astype(jnp.int32) * 2 + group % 2


def third_border(s, groups, side, adjoint, even, odd, sides, edges):
    prev, next_ = arrivals(side, even, odd)
    slot = slot_of(groups[s], side)

    @pl.when(s == 0)
    def start():
        clear(edges)

    for k in range(0, SX, ROWS):
        group = slice(k, k + ROWS)
        for h in range(2):
            value = {r: adjoint[0, h, every(k, r), :] + prev[0, r, group, half(h)] for r in (0, 1)}
            value.update({6 + r: adjoint[0, h, every(k, 6 + r), :] + next_[0, r, group, half(h)] for r in (0, 1)})
            speed = dict(zip((0, 1, 6, 7), (sides[0, i, group, half(h)] for i in range(4))))
            pos = {r: jnp.maximum(speed[r], 0.0) * value[r] for r in (0, 1, 7)}
            neg = {r: jnp.minimum(speed[r], 0.0) * value[r] for r in (0, 6, 7)}
            for ref, r, change in outgoing(pos, neg):
                at = (2 * ref + r) * SX + k
                edges[slot, at:at + ROWS, half(h)] += change


def fourth_kernel(low, high, near, s, groups, side, adjoint, even, odd, weights, sums,
                  value, pos_pad, neg_pad, lhs, along, velocity):
    prev, next_ = arrivals(side, even, odd)
    slot = slot_of(groups[s], side)

    @pl.when(s == 0)
    def start():
        for ref in (sums, pos_pad, neg_pad):
            clear(ref)

    base, stop = max(low - 8, 0), min(high + 8, SX)

    def copy(k):
        for h in range(2):
            value[h, of(k), :] = adjoint[0, h, of(base + k), :]

    loop(stop - base, copy)
    for x in range(base, stop, ROWS):
        for h in range(2):
            for r in range(2):
                value[h, every(x - base, r), :] += prev[0, r, x:x + ROWS, half(h)]
                value[h, every(x - base, 6 + r), :] += next_[0, r, x:x + ROWS, half(h)]

    def emit(h, x, result):
        sums[slot, x - low, :, half(h)] += result

    retreat(low, high, value, base, near, velocity, emit, weights, pos_pad, neg_pad, lhs, along)


def call(body, scalars, ins, outs, arrays, scratch, velocity=None, part=(0, SX), nbytes=40_000_000):
    fixed = len(scalars)
    views = [view for view, _ in ins] + [view for _, view in outs]
    low, high = part
    in_specs = [pl.BlockSpec(memory_space=pltpu.SMEM)] * fixed
    in_specs += [pl.BlockSpec(memory_space=space) for _, space in ins]
    if velocity is not None:
        scratch = scratch + [pltpu.VMEM((2, 3, high - low, ROWS, NZ), jnp.int32), pltpu.SemaphoreType.DMA((2,))]
        in_specs += [pl.BlockSpec(memory_space=pltpu.HBM)]
        arrays = arrays + (velocity,)

    def kernel(*refs):
        refs = list(refs)
        more = {}
        if velocity is not None:
            source = refs.pop(fixed + len(ins))
            buffer, sem = refs[-2:]
            refs = refs[:-2]

            def fetch(s, slot):
                return pltpu.make_async_copy(source.at[s, :, pl.ds(low, high - low)], buffer.at[slot], sem.at[slot])

            fetch(0, 0).start()

        def one(s, carry):
            seen = [view(ref, s, refs[0]) for view, ref in zip(views, refs[fixed:])]
            if velocity is not None:
                slot = s % 2

                @pl.when(s + 1 < SUBS)
                def ahead():
                    fetch(s + 1, 1 - slot).start()

                fetch(s, slot).wait()
                more["velocity"] = buffer.at[pl.ds(slot, 1)]
            body(s, *refs[:fixed], *seen, *refs[fixed + len(views):], **more)
            return carry

        lax.fori_loop(0, SUBS, one, 0)

    return pl.pallas_call(
        kernel,
        in_specs=in_specs,
        out_specs=[pl.BlockSpec(memory_space=pltpu.VMEM)] * len(outs),
        out_shape=[jax.ShapeDtypeStruct(shape.shape, shape.dtype) for shape, _ in outs],
        scratch_shapes=scratch,
        compiler_params=pltpu.CompilerParams(vmem_limit_bytes=VMEM if velocity is None else STREAMING),
        cost_estimate=pl.CostEstimate(flops=nbytes, bytes_accessed=nbytes, transcendentals=0),
    )(*scalars, *arrays)


def everything(ref, s, groups):
    return ref


def subject(ref, s, groups):
    return ref.at[pl.ds(s, 1)]


def pair(ref, s, groups):
    return ref.at[:, pl.ds(s, 1)]


def swap(even, odd, count):
    pairs = [[(i, i + 1) for i in range(first, count - 1, 2)] for first in (0, 1)]
    both_ways = [[(a, b) for a, b in part] + [(b, a) for a, b in part] for part in pairs]
    odd = lax.ppermute(odd, "tile", both_ways[1])
    even = lax.ppermute(even, "tile", both_ways[0])
    return even, odd


def shards(template, images, velocity, groups):
    count = lax.axis_size("tile")
    place = lax.axis_index("subj")
    core, high_y = place % 2, place // 2
    some = GROUPS // 2
    core_pairs = [(0, 1), (1, 0), (2, 3), (3, 2)]
    y_pairs = [(0, 2), (2, 0), (1, 3), (3, 1)]
    is_odd = lax.axis_index("tile") % 2 == 1
    side = jnp.stack([core, high_y, is_odd]).astype(jnp.int32)
    plus, minus = stencil(PLUS), stencil(MINUS)
    onward = np.concatenate([plus.T, minus.T], axis=1)
    onward = jnp.asarray(np.concatenate([onward, onward], axis=0), jnp.bfloat16)
    backward = jnp.asarray(np.concatenate([plus, plus, minus, minus], axis=0), jnp.bfloat16)
    f32, bf16 = jnp.float32, jnp.bfloat16
    vmem = lambda shape, dtype=f32: pltpu.VMEM(shape, dtype)
    shape = jax.ShapeDtypeStruct
    field = shape((SUBS, 2, SX * ROWS, HALF), f32)
    edge = shape((SUBS, 2, SX, NZ), f32)
    edges_both = shape((2, SUBS, 2, SX, NZ), f32)
    one, all_ = (subject, pltpu.VMEM), (everything, pltpu.VMEM)
    rows = SX * ROWS

    mine = lax.dynamic_slice_in_dim(template, core * some, some, axis=0)
    ends = jnp.swapaxes(jnp.concatenate([mine[:, :, 0:2], mine[:, :, 6:8]], axis=2), 1, 2)
    up, down = ends[:, 0:2], ends[:, 2:4]
    even_own, odd_own = swap(jnp.where(is_odd, up, down), jnp.where(is_odd, down, up), count)

    moved, sides = call(
        first_kernel,
        (groups,),
        [(lambda ref, s, g: ref.at[pl.ds(g[s], 1)], pltpu.VMEM), all_],
        [(field, subject), (shape((SUBS, 4, SX, NZ), f32), subject)],
        (template, onward),
        [vmem(pad_rows(SX + 4)), vmem((2, rows, HALF)), vmem((rows, 2 * NZ), bf16), vmem((rows, 2 * NZ))],
        velocity=velocity,
    )
    even_own, odd_own, sides = lax.optimization_barrier((even_own, odd_own, sides))
    even_other = lax.ppermute(even_own, "subj", core_pairs)
    odd_other = lax.ppermute(odd_own, "subj", core_pairs)
    of_group = (lambda ref, s, g: ref.at[pl.ds(g[s] % some, 1)], pltpu.VMEM)
    (both,) = call(
        first_border,
        (groups, side),
        [one] + [of_group] * 4 + [one],
        [(edges_both, pair)],
        (moved, even_own, even_other, odd_own, odd_other, sides),
        [],
    )
    even, odd = swap(both[0], both[1], count)
    (residual,) = call(
        second_kernel,
        (groups, side),
        [one, (pair, pltpu.VMEM), one, all_],
        [(field, subject)],
        (moved, both, images, onward),
        [vmem(pad_rows(SX + 4)), vmem((rows, 2 * NZ), bf16), vmem((rows, 2 * NZ))],
        velocity=velocity,
    )
    top, bottom, both = call(
        second_border,
        (groups, side),
        [one] * 4,
        [(edge, subject)] * 2 + [(edges_both, pair)],
        (residual, even, odd, sides),
        [],
    )
    even, odd = swap(both[0], both[1], count)
    (adjoint,) = call(
        third_kernel,
        (groups,),
        [one] * 3 + [all_],
        [(field, subject)],
        (residual, top, bottom, backward),
        [
            vmem((2, rows, HALF)),
            vmem(pad_rows(SX + 8)),
            vmem(pad_rows(SX + 8)),
            vmem((rows, 4 * NZ), bf16),
            vmem((rows, NZ)),
        ],
        velocity=velocity,
    )

    (edges,) = call(
        third_border,
        (groups, side),
        [one] * 4,
        [(shape((GROUPS, 4 * SX, NZ), f32), everything)],
        (adjoint, even, odd, sides),
        [],
    )
    edges4 = edges[some:] + lax.ppermute(edges[:some], "subj", core_pairs)
    adjoint, edges4 = lax.optimization_barrier((adjoint, edges4))
    up, down = edges4[:, :2 * SX], edges4[:, 2 * SX:]
    even_ends, odd_ends = swap(jnp.where(is_odd, up, down), jnp.where(is_odd, down, up), count)
    (sums,) = call(
        functools.partial(fourth_kernel, 0, SX, 0),
        (groups, side),
        [one] * 3 + [all_],
        [(shape((GROUPS, SX, ROWS, NZ), f32), everything)],
        (adjoint, even, odd, backward),
        [
            vmem((2, rows, HALF)),
            vmem(pad_rows(SX + 8)),
            vmem(pad_rows(SX + 8)),
            vmem((rows, 4 * NZ), bf16),
            vmem((rows, NZ)),
        ],
        velocity=velocity,
    )
    sums, even_ends, odd_ends = lax.optimization_barrier((sums, even_ends, odd_ends))
    arrived = lax.ppermute(sums[:some], "subj", core_pairs)
    middle = jnp.zeros((some, SX, ROWS - 4, NZ), f32)
    from_prev, from_next = jnp.where(is_odd, even_ends, odd_ends), jnp.where(is_odd, odd_ends, even_ends)
    from_prev, from_next = (jnp.swapaxes(e.reshape(some, 2, SX, NZ), 1, 2) for e in (from_prev, from_next))
    sums4 = sums[some:] + jnp.concatenate([from_prev, middle, from_next], axis=2)
    sums4 = sums4 + arrived
    return sums4[2:] + lax.ppermute(sums4[:2], "subj", y_pairs)


def solution(mesh):
    in_specs = (
        P(None, None, "tile", None),
        P("subj", None, "tile", None),
        P("subj", None, None, "tile", None),
        P("subj"),
    )
    out_specs = P("subj", None, "tile", None)
    return jax.shard_map(shards, mesh=mesh, in_specs=in_specs, out_specs=out_specs, check_vma=False)
```
